32 devices in a mesh: dom: 8 (over z, x), tp: 4 (over y, core).
Axes of the slice: x: 2, y: 2, z: 4, core: 2. Of those that a mesh axis runs over, the one named last changes fastest.
Arguments:
- hidden: bfloat16 [4, 8, 256, 8192], P(None, 'dom', None, 'tp')
- fc2_weight: bfloat16 [8192, 8192], P('tp')
- fc2_bias: bfloat16 [8192], replicated, may hold values from -6 to 6
- norm_gain: bfloat16 [8192], replicated, may hold values from 0.099609375 to 1.8984375
- kv_weight: bfloat16 [8192, 2048], P('tp'), may hold values from -0.09375 to 0.09375
- kv_bias: bfloat16 [2048], replicated, may hold values from -3 to 3
- tiles_per_request: int32 [16], replicated, may hold values from 0 to 8, as said below
- request_group: int32 [16], replicated, may hold values from 0 to 7, as said below
- text_lengths: int32 [16], replicated, may hold values from 16 to 2047
Outputs:
- kv_cache: bfloat16 [16384, 2048], P('dom', 'tp')
The draws below stay inside these ranges and needn't reach their ends.
Inputs may be any that keep to these rules, and one draw needn't show every extreme that they name: `tiles_per_request`: sums to 32; the requests of one prefill group hold at most 8 tiles together, and some group holds exactly that many. `request_group`: never falls from one request to the next; every prefill group has at least one request.
All inputs are finite; a program needn't handle non-finite values.
Results may differ from the reference program's by a relative error of at most 0.017.
Values may be sent and summed in bfloat16 or wider, within the bound.
A program may use at most 192 MiB of HBM per device.

```python
import math
import jax
import jax.numpy as jnp
from jax import lax

D = 8192
HEAD = 128
ROWS_TILE = 256
TILE_ENC = 4
PRE_TILES = 8
REQUESTS = 16
KV_COLS = 2048
N_DOM = 8
N_TP = 4


def pair_deltas(key, forced, top_shift):
    half_count = N_DOM // 2
    sub_keys = jax.random.split(key, 3)
    shuffled = jax.random.permutation(sub_keys[0], N_DOM).astype(jnp.int32)
    group_ids = jnp.arange(N_DOM, dtype=jnp.int32)
    places = jnp.sum((shuffled[None, :] == group_ids[:, None]).astype(jnp.int32) * group_ids[None, :], axis=1).astype(jnp.int32)
    pair_of = places // 2
    sign_of = 1 - 2 * (places % 2)
    shifts = jax.random.randint(sub_keys[1], (half_count,), 0, top_shift + 1)
    flipped = jax.random.randint(sub_keys[2], (half_count,), 0, 2)
    direction = 1 - 2 * flipped
    pair_ids = jnp.arange(half_count, dtype=jnp.int32)
    forced_pair = jnp.sum(jnp.where(group_ids == forced, pair_of, 0)).astype(jnp.int32)
    forced_sign = jnp.sum(jnp.where(group_ids == forced, sign_of, 0)).astype(jnp.int32)
    shifts = jnp.where(pair_ids == forced_pair, top_shift, shifts)
    direction = jnp.where(pair_ids == forced_pair, forced_sign, direction)
    pair_hits = (pair_of[:, None] == pair_ids[None, :]).astype(jnp.int32)
    group_shift = jnp.sum(pair_hits * (direction * shifts)[None, :], axis=1).astype(jnp.int32)
    return ((sign_of * group_shift).astype(jnp.int32), pair_hits, sign_of)


def joint_routing(key):
    half_count = N_DOM // 2
    sub_keys = jax.random.split(jax.random.fold_in(key, 101), 6)
    forced = jax.random.randint(sub_keys[0], (), 0, N_DOM)
    first_share = TILE_ENC // 2
    second_share = TILE_ENC - first_share
    first_delta, pair_hits, sign_of = pair_deltas(sub_keys[1], forced, first_share)
    second_delta, unused_hits, unused_sign = pair_deltas(sub_keys[2], forced, second_share)
    counts = (TILE_ENC + first_delta + second_delta).astype(jnp.int32)
    extras = jax.random.randint(sub_keys[3], (half_count,), -1, 2)
    group_extra = jnp.sum(pair_hits * extras[None, :], axis=1).astype(jnp.int32)
    request_counts = (2 + sign_of * group_extra).astype(jnp.int32)
    request_ends = jnp.cumsum(request_counts).astype(jnp.int32)
    request_starts = request_ends - request_counts
    request_ids = jnp.arange(REQUESTS, dtype=jnp.int32)
    group_of = jnp.sum((request_ends[None, :] <= request_ids[:, None]).astype(jnp.int32), axis=1).astype(jnp.int32)
    index_in = request_ids - request_starts[group_of]
    first_cut = jax.random.randint(sub_keys[4], (N_DOM,), 0, counts + 1)
    second_cut = jax.random.randint(sub_keys[5], (N_DOM,), 0, counts + 1)
    low_cut = jnp.minimum(first_cut, second_cut)
    high_cut = jnp.maximum(first_cut, second_cut)
    edge_one = jnp.where(request_counts >= 2, low_cut, counts)
    edge_two = jnp.where(request_counts >= 3, high_cut, counts)
    cut_edges = jnp.stack([jnp.zeros_like(counts), edge_one, edge_two, counts], axis=1)
    tile_sizes = cut_edges[group_of, index_in + 1] - cut_edges[group_of, index_in]
    return (tile_sizes.astype(jnp.int32), group_of.astype(jnp.int32))


def draw_tiles_per_request(key, part):
    shared = joint_routing(key)
    return shared[0]


def draw_request_group(key, part):
    shared = joint_routing(key)
    return shared[1]


def draw_hidden(key, part):
    key = jax.random.fold_in(key, 11)
    first_key, second_key = jax.random.split(key)
    shape = (TILE_ENC, N_DOM, ROWS_TILE, D)
    base = jax.random.normal(first_key, shape, jnp.float32)
    scale = 10.0 ** jax.random.uniform(second_key, (TILE_ENC, N_DOM, ROWS_TILE, 1), jnp.float32, -0.5, 0.5)
    return (base * scale).astype(jnp.bfloat16)


def draw_fc2_weight(key, part):
    key = jax.random.fold_in(key, 13)
    first_key, second_key = jax.random.split(key)
    place = jnp.arange(D, dtype=jnp.float32) / D - 0.5
    base = jax.random.normal(first_key, (D, D), jnp.float32)
    spread = 10.0 ** jax.random.uniform(second_key, (1, D), jnp.float32, -0.5, 0.5)
    trend = 3.0 ** place
    return (base * spread * trend[None, :] / math.sqrt(D)).astype(jnp.bfloat16)


def set_ends(result, key, least, largest):
    longest = result.shape.index(max(result.shape))
    spots = []
    for shift in (0, 1):
        where = [jax.random.randint(jax.random.fold_in(key, axis), (), 0, length) for axis, length in enumerate(result.shape)]
        where[longest] = (where[longest] + shift) % result.shape[longest]
        spots.append(tuple(where))
    return result.at[spots[0]].set(least).at[spots[1]].set(largest)


def raised(values, stream_key, source, target, parts, factor):
    def block_of(dim):
        return (jnp.arange(values.shape[dim]) // (values.shape[dim] // parts)).reshape((-1,) + (1,) * (values.ndim - 1 - dim))

    near = jax.random.permutation(stream_key, parts)[block_of(target)]
    far = (block_of(target) + parts // 2) % parts
    return jnp.where((block_of(source) == near) | (block_of(source) == far), factor * values, values)


def level_of(own_key, extent, pieces, least, high):
    level, own = 1.0, jax.random.fold_in(own_key, 6)
    for axis_at, parts in pieces:
        heights = jnp.exp(jax.random.uniform(jax.random.fold_in(own, axis_at), (parts,), jnp.float32, least / len(pieces), high / len(pieces)))
        level = level * jnp.repeat(heights, extent[axis_at] // parts).reshape([-1 if axis == axis_at else 1 for axis in range(len(extent))])
    return level


def noise(key, shape, scale, reach, shards=(), kind=jnp.bfloat16):
    entries = scale * jax.random.normal(key, shape, jnp.float32)
    if shards:
        entries = entries * level_of(key, shape, shards, -0.22, 0.18)
    return jnp.clip(entries, -reach, reach).astype(kind)


def gaussian_with(key, dims, scale, limit, cuts, heavy, held_as=jnp.bfloat16):
    drawn = scale * jax.random.normal(key, dims, jnp.float32)
    if cuts:
        drawn = drawn * level_of(key, dims, cuts, -0.22, 0.18)
    return jnp.clip(raised(drawn, jax.random.fold_in(key, 3), *heavy), -limit, limit).astype(held_as)


def setup_inputs(seed: int = 0) -> dict:
    splits = jax.random.split(jax.random.key(seed), 10)
    hidden = draw_hidden(jax.random.fold_in(splits[9], 71), 0)
    fc2_weight = draw_fc2_weight(jax.random.fold_in(splits[9], 71), 0)
    fc2_bias = noise(splits[2], (D,), 1.0, 6.0)
    norm_gain = jnp.clip(1.0 + 0.18 * jax.random.normal(splits[3], (D,), jnp.float32), 0.099609375, 1.8984375).astype(jnp.bfloat16)
    kv_weight = gaussian_with(splits[4], (D, KV_COLS), D ** -0.5, 0.09375, ((0, 4),), (0, 1, 4, 2.0))
    kv_bias = noise(splits[5], (KV_COLS,), 0.5, 3.0)
    tiles_per_request = draw_tiles_per_request(jax.random.fold_in(splits[9], 71), 0)
    request_group = draw_request_group(jax.random.fold_in(splits[9], 71), 0)
    text_lengths = set_ends(jax.random.randint(splits[8], (REQUESTS,), 16, 2048), jax.random.fold_in(splits[8], 1), 16, 2047).astype(jnp.int32)
    return dict(hidden=hidden, fc2_weight=fc2_weight, fc2_bias=fc2_bias, norm_gain=norm_gain, kv_weight=kv_weight, kv_bias=kv_bias, tiles_per_request=tiles_per_request, request_group=request_group, text_lengths=text_lengths)


EPS = 1e-06
ROPE_BASE = 1000000.0

def tile_plan(tiles_per_request, request_group, text_lengths, tile_count, group_count, rows_tile):
    request_count = tiles_per_request.shape[0]
    ends = jnp.cumsum(tiles_per_request).astype(jnp.int32)
    starts = ends - tiles_per_request.astype(jnp.int32)
    tile_ids = jnp.arange(tile_count, dtype=jnp.int32)
    owner = lax.optimization_barrier(jnp.sum((ends[None, :] <= tile_ids[:, None]).astype(jnp.int32), axis=1)).astype(jnp.int32)
    member = (owner[:, None] == jnp.arange(request_count, dtype=jnp.int32)[None, :]).astype(jnp.int32)
    start_of = lax.optimization_barrier(jnp.sum(member * starts[None, :], axis=1)).astype(jnp.int32)
    group_of = lax.optimization_barrier(jnp.sum(member * request_group[None, :], axis=1)).astype(jnp.int32)
    text_of = lax.optimization_barrier(jnp.sum(member * text_lengths[None, :], axis=1)).astype(jnp.int32)
    group_ids = jnp.arange(group_count, dtype=jnp.int32)
    same_group = (request_group[None, :] == group_ids[:, None]).astype(jnp.int32)
    below_group = (request_group[None, :] < group_ids[:, None]).astype(jnp.int32)
    counts = lax.optimization_barrier(jnp.sum(same_group * tiles_per_request[None, :], axis=1)).astype(jnp.int32)
    firsts = lax.optimization_barrier(jnp.sum(below_group * tiles_per_request[None, :], axis=1)).astype(jnp.int32)
    first_of = lax.optimization_barrier(jnp.sum((group_of[:, None] == group_ids[None, :]).astype(jnp.int32) * firsts[None, :], axis=1)).astype(jnp.int32)
    slot_of = tile_ids - first_of
    base_of = text_of + (tile_ids - start_of) * rows_tile
    return (group_of, slot_of, base_of, counts, firsts)

def rotate_heads(values, positions, head_size):
    row_count, col_count = values.shape
    grid = values.reshape(row_count, col_count // head_size, head_size)
    half_size = head_size // 2
    freqs = ROPE_BASE ** (-jnp.arange(half_size, dtype=jnp.float32) * 2.0 / head_size)
    angles = positions.astype(jnp.float32)[:, None] * freqs[None, :]
    cosine = jnp.concatenate([jnp.cos(angles), jnp.cos(angles)], axis=1)[:, None, :]
    sine = jnp.concatenate([jnp.sin(angles), jnp.sin(angles)], axis=1)[:, None, :]
    turned = jnp.concatenate([-grid[..., half_size:], grid[..., :half_size]], axis=-1)
    return (grid * cosine + turned * sine).reshape(row_count, col_count)

def block_sum(left, right, block_width, block_count):

    def add_block(block_index, total):
        offset = (block_index * block_width).astype(jnp.int32)
        left_part = lax.dynamic_slice_in_dim(left, offset, block_width, 1)
        right_part = lax.dynamic_slice_in_dim(right, offset, block_width, 0)
        product = jnp.dot(left_part, right_part, preferred_element_type=jnp.float32)
        rounded = lax.optimization_barrier(product.astype(jnp.bfloat16))
        return total + rounded.astype(jnp.float32)
    start = jnp.zeros((left.shape[0], right.shape[1]), jnp.float32)
    return lax.fori_loop(0, block_count, add_block, start)

def reference(hidden, fc2_weight, fc2_bias, norm_gain, kv_weight, kv_bias, tiles_per_request, request_group, text_lengths):
    tile_count = TILE_ENC * N_DOM
    row_total = tile_count * ROWS_TILE
    block_width = D // N_TP
    tile_rows = hidden.reshape(row_total, D)
    projected = (block_sum(tile_rows, fc2_weight, block_width, N_TP) + fc2_bias.astype(jnp.float32)[None, :]).astype(jnp.bfloat16)
    widened = projected.astype(jnp.float32)
    scale = lax.rsqrt(lax.optimization_barrier(jnp.mean(widened * widened, axis=1, keepdims=True)) + EPS)
    normed = (widened * scale * norm_gain.astype(jnp.float32)[None, :]).astype(jnp.bfloat16)
    raw = block_sum(normed, kv_weight, block_width, N_TP) + kv_bias.astype(jnp.float32)[None, :]
    group_of, slot_of, base_of, counts, firsts = tile_plan(tiles_per_request, request_group, text_lengths, tile_count, N_DOM, ROWS_TILE)
    positions = (base_of[:, None] + jnp.arange(ROWS_TILE, dtype=jnp.int32)[None, :]).reshape(row_total)
    key_width = KV_COLS // 2
    keys = rotate_heads(raw[:, :key_width], positions, HEAD)
    rotated = jnp.concatenate([keys, raw[:, key_width:]], axis=1)
    cache = rotated.astype(jnp.bfloat16).reshape(tile_count, ROWS_TILE, KV_COLS)
    placed = jnp.zeros((N_DOM, PRE_TILES, ROWS_TILE, KV_COLS), jnp.bfloat16).at[group_of, slot_of].set(cache)
    return placed.reshape(N_DOM * PRE_TILES * ROWS_TILE, KV_COLS)
```

```python
import functools

import jax
import jax.numpy as jnp
from jax import lax
from jax.experimental import pallas as pl
from jax.experimental.pallas import tpu as pltpu
from jax.sharding import PartitionSpec as P

HEAD = 128


EPS = 1e-06
ROPE_BASE = 1000000.0


def tile_plan(tiles_per_request, request_group, text_lengths, tile_count, group_count, rows_tile):
    request_count = tiles_per_request.shape[0]
    ends = jnp.cumsum(tiles_per_request)
    starts = ends - tiles_per_request
    tile_ids = jnp.arange(tile_count, dtype=jnp.int32)
    owner = jnp.sum((ends[None, :] <= tile_ids[:, None]).astype(jnp.int32), axis=1)
    member = (owner[:, None] == jnp.arange(request_count, dtype=jnp.int32)[None, :]).astype(
        jnp.int32
    )
    start_of = jnp.sum(member * starts[None, :], axis=1)
    group_of = jnp.sum(member * request_group[None, :], axis=1)
    text_of = jnp.sum(member * text_lengths[None, :], axis=1)
    group_ids = jnp.arange(group_count, dtype=jnp.int32)
    same_group = (request_group[None, :] == group_ids[:, None]).astype(jnp.int32)
    below_group = (request_group[None, :] < group_ids[:, None]).astype(jnp.int32)
    counts = jnp.sum(same_group * tiles_per_request[None, :], axis=1)
    firsts = jnp.sum(below_group * tiles_per_request[None, :], axis=1)
    first_of = jnp.sum(
        (group_of[:, None] == group_ids[None, :]).astype(jnp.int32) * firsts[None, :], axis=1
    )
    slot_of = tile_ids - first_of
    base_of = text_of + (tile_ids - start_of) * rows_tile
    return (group_of, slot_of, base_of, counts, firsts)


def rotate_heads(values, positions, head_size):
    row_count, col_count = values.shape
    grid = values.reshape(row_count, col_count // head_size, head_size)
    half_size = head_size // 2
    freqs = ROPE_BASE ** (-jnp.arange(half_size, dtype=jnp.float32) * 2.0 / head_size)
    angles = positions.astype(jnp.float32)[:, None] * freqs[None, :]
    cosine = jnp.concatenate([jnp.cos(angles), jnp.cos(angles)], axis=1)[:, None, :]
    sine = jnp.concatenate([jnp.sin(angles), jnp.sin(angles)], axis=1)[:, None, :]
    turned = jnp.concatenate([-grid[..., half_size:], grid[..., :half_size]], axis=-1)
    return (grid * cosine + turned * sine).reshape(row_count, col_count)


def lookup(table, wanted):
    table_ids = jnp.arange(table.shape[0], dtype=jnp.int32)
    hits = (wanted[:, None] == table_ids[None, :]).astype(jnp.int32)
    return jnp.sum(hits * table[None, :], axis=1)


def pick_rows(picker, payload):
    return jnp.dot(picker, payload, preferred_element_type=jnp.float32).astype(jnp.bfloat16)


def finish_cache(summed, kv_bias, positions, lane_index, lane_cols, cache_cols):
    bias_part = lax.dynamic_slice_in_dim(kv_bias, lane_index * lane_cols, lane_cols).astype(
        jnp.float32
    )
    raw = summed + bias_part[None, :]
    turned = rotate_heads(raw, positions, HEAD)
    is_key = lane_index * lane_cols < cache_cols // 2
    return jnp.where(is_key, turned, raw).astype(jnp.bfloat16)


def body(
    hidden,
    fc2_weight,
    fc2_bias,
    norm_gain,
    kv_weight,
    kv_bias,
    tiles_per_request,
    request_group,
    text_lengths,
):
    group_count = lax.axis_size("dom")
    lane_count = lax.axis_size("tp")
    group_index = lax.axis_index("dom")
    lane_index = lax.axis_index("tp")
    local_tiles = hidden.shape[0]
    rows_tile = hidden.shape[2]
    local_width = hidden.shape[3]
    model_width = fc2_weight.shape[1]
    cache_cols = kv_weight.shape[1]
    lane_cols = cache_cols // lane_count
    pre_tiles = 2 * local_tiles
    tile_count = local_tiles * group_count
    group_of, slot_of, base_of, counts, firsts = tile_plan(
        tiles_per_request, request_group, text_lengths, tile_count, group_count, rows_tile
    )
    tile_rows = hidden.reshape(local_tiles * rows_tile, local_width)
    partial_value = jnp.dot(tile_rows, fc2_weight, preferred_element_type=jnp.float32).reshape(
        local_tiles, rows_tile, model_width
    )
    summed_cols = lax.psum_scatter(
        partial_value.astype(jnp.bfloat16), "tp", scatter_dimension=2, tiled=True
    ).astype(jnp.float32)
    bias_part = lax.dynamic_slice_in_dim(fc2_bias, lane_index * local_width, local_width).astype(
        jnp.float32
    )
    gain_part = lax.dynamic_slice_in_dim(norm_gain, lane_index * local_width, local_width).astype(
        jnp.float32
    )
    projected = (summed_cols + bias_part[None, None, :]).astype(jnp.bfloat16)
    widened = projected.astype(jnp.float32)
    squares = lax.psum(jnp.sum(widened * widened, axis=2), "tp")
    scale = lax.rsqrt(squares / model_width + EPS)[..., None]
    normed = (widened * scale * gain_part[None, None, :]).astype(jnp.bfloat16)
    group_ids = jnp.arange(group_count, dtype=jnp.int32)
    mine = jnp.arange(local_tiles, dtype=jnp.int32) * group_count + group_index
    mine_group = lookup(group_of, mine)
    send_picker = (group_ids[:, None] == mine_group[None, :]).astype(jnp.bfloat16)
    slot_ids = jnp.arange(pre_tiles, dtype=jnp.int32)
    my_count = lookup(counts, jnp.full((1,), group_index, jnp.int32))[0]
    my_first = lookup(firsts, jnp.full((1,), group_index, jnp.int32))[0]
    wanted = my_first + slot_ids
    valid = slot_ids < my_count
    source = wanted % group_count
    take_picker = jnp.logical_and(source[:, None] == group_ids[None, :], valid[:, None]).astype(
        jnp.bfloat16
    )
    row_ids = jnp.arange(rows_tile, dtype=jnp.int32)
    partial_kv = jnp.dot(
        normed.reshape(local_tiles * rows_tile, local_width),
        kv_weight,
        preferred_element_type=jnp.float32,
    )
    summed_kv = lax.psum_scatter(
        partial_kv.astype(jnp.bfloat16), "tp", scatter_dimension=1, tiled=True
    ).astype(jnp.float32)
    mine_positions = (lookup(base_of, mine)[:, None] + row_ids[None, :]).reshape(
        local_tiles * rows_tile
    )
    cache = finish_cache(summed_kv, kv_bias, mine_positions, lane_index, lane_cols, cache_cols)
    outgoing = pick_rows(send_picker, cache.reshape(local_tiles, rows_tile * lane_cols))
    arrived = lax.all_to_all(
        outgoing.reshape(group_count, rows_tile, lane_cols),
        "dom",
        split_axis=0,
        concat_axis=0,
        tiled=True,
    )
    placed = pick_rows(take_picker, arrived.reshape(group_count, rows_tile * lane_cols))
    return placed.reshape(pre_tiles * rows_tile, lane_cols)


ROW_CHUNKS = 4
COL_CHUNKS = 8
W_SLOTS = 3
C_SLOTS = 4
Y_SLOTS = 8
LAG = 4
E_LAG = 1
F_LAG = 4


def fused_kernel(
    groups,
    requests,
    x,
    w,
    b2,
    gain,
    kvw,
    kvb,
    tpr,
    rg,
    tl,
    freq,
    out,
    xbuf,
    wbuf,
    kvbuf,
    b2f,
    gf,
    kvbf,
    csend,
    crecv,
    own,
    ysend,
    yrecv,
    mine,
    kvacc,
    sqacc,
    kcsend,
    kcrecv,
    kysend,
    kyrecv,
    kmine,
    sqsend,
    sqcrecv,
    sqysend,
    sqyrecv,
    cos_t,
    sin_t,
    asend,
    arecv,
    xsem,
    wsem,
    kvsem,
    cs_sem,
    cr_sem,
    ys_sem,
    yr_sem,
    ks_sem,
    kr_sem,
    kys_sem,
    kyr_sem,
    as_sem,
    ar_sem,
):
    tiles, rows_tile, width = x.shape
    R, S = ROW_CHUNKS, COL_CHUNKS
    N = R * S
    sub = rows_tile // R
    M = tiles * sub
    model = w.shape[1]
    wc = width // S
    kc = kvw.shape[1] // 4
    t = lax.axis_index("tp")
    d = lax.axis_index("dom")
    c = lax.rem(t, 2)
    y = t // 2
    sib = t + 1 - 2 * c
    opp = t + 2 - 4 * y
    oy, oc = 1 - y, 1 - c
    owners = (2 * oy + oc, 2 * y + oc, 2 * oy + c, t)
    f32, bf16 = jnp.float32, jnp.bfloat16

    def x_copies(r):
        return [
            pltpu.make_async_copy(
                x.at[j, pl.ds(r * sub, sub), :], xbuf.at[r, pl.ds(j * sub, sub), :], xsem.at[r, j]
            )
            for j in range(tiles)
        ]

    def w_copies(n):
        s = lax.rem(n, S)
        slot = lax.rem(n, W_SLOTS)
        return [
            pltpu.make_async_copy(
                w.at[:, pl.ds(pl.multiple_of(owners[p] * width + s * wc, wc), wc)],
                wbuf.at[slot, p],
                wsem.at[slot, p],
            )
            for p in range(4)
        ]

    def kv_copies():
        return [
            pltpu.make_async_copy(
                kvw.at[:, pl.ds(pl.multiple_of(owners[p] * kc, kc), kc)],
                kvbuf.at[p],
                kvsem.at[p],
            )
            for p in range(4)
        ]

    for cp in x_copies(0):
        cp.start()
    for n in range(W_SLOTS):
        for cp in w_copies(jnp.int32(n)):
            cp.start()
    for r in range(1, R):
        for cp in x_copies(r):
            cp.start()
    for cp in kv_copies():
        cp.start()

    barrier = pltpu.get_barrier_semaphore()
    pl.semaphore_signal(barrier, inc=1, device_id={"tp": sib}, device_id_type=pl.DeviceIdType.MESH)
    pl.semaphore_signal(barrier, inc=1, device_id={"tp": opp}, device_id_type=pl.DeviceIdType.MESH)
    for k in range(1, groups):
        pl.semaphore_signal(
            barrier,
            inc=1,
            device_id={"dom": lax.rem(d + k, groups)},
            device_id_type=pl.DeviceIdType.MESH,
        )

    b2f[...] = b2[...].astype(f32)
    gf[...] = gain[...].astype(f32)
    kvbf[...] = kvb[...].astype(f32)

    tile_group = []
    tile_base = []
    for j in range(tiles):
        tid = j * groups + d
        end = jnp.int32(0)
        grp = jnp.int32(0)
        base = jnp.int32(0)
        for q in range(requests):
            start = end
            end = end + tpr[q]
            hit = jnp.logical_and(start <= tid, tid < end)
            grp = grp + jnp.where(hit, rg[q], 0)
            base = base + jnp.where(hit, tl[q] + (tid - start) * rows_tile, 0)
        tile_group.append(grp)
        tile_base.append(base)
    first = jnp.int32(0)
    count = jnp.int32(0)
    for q in range(requests):
        first = first + jnp.where(rg[q] < d, tpr[q], 0)
        count = count + jnp.where(rg[q] == d, tpr[q], 0)
    is_key = (t * kc < 2 * kc).astype(jnp.int32)

    def remote(src, dst, send, recv, axis, target):
        return pltpu.make_async_remote_copy(
            src_ref=src,
            dst_ref=dst,
            send_sem=send,
            recv_sem=recv,
            device_id={axis: target},
            device_id_type=pl.DeviceIdType.MESH,
        )

    def c_copy(n):
        slot = lax.rem(n, C_SLOTS)
        return remote(csend.at[slot], crecv.at[n], cs_sem.at[slot], cr_sem.at[n], "tp", sib)

    def y_copy(n):
        slot = lax.rem(n, Y_SLOTS)
        return remote(ysend.at[slot], yrecv.at[n], ys_sem.at[slot], yr_sem.at[n], "tp", opp)

    def kc_copy(r):
        return remote(kcsend.at[r], kcrecv.at[r], ks_sem.at[0, r], kr_sem.at[0, r], "tp", sib)

    def sqc_copy(r):
        return remote(sqsend.at[r], sqcrecv.at[r], ks_sem.at[1, r], kr_sem.at[1, r], "tp", sib)

    def ky_copy(r):
        return remote(kysend.at[r], kyrecv.at[r], kys_sem.at[0, r], kyr_sem.at[0, r], "tp", opp)

    def sqy_copy(r):
        return remote(sqysend.at[r], sqyrecv.at[r], kys_sem.at[1, r], kyr_sem.at[1, r], "tp", opp)

    def a_send(r, k):
        return remote(
            asend.at[r, k],
            arecv.at[d, pl.ds(pl.multiple_of(r * sub, sub), sub), :],
            as_sem.at[r, k],
            ar_sem.at[r, k],
            "dom",
            lax.rem(d + k, groups),
        )

    def a_recv(r, k):
        return remote(
            asend.at[r, k],
            arecv.at[lax.rem(d + groups - k, groups), pl.ds(pl.multiple_of(r * sub, sub), sub), :],
            as_sem.at[r, k],
            ar_sem.at[r, k],
            "dom",
            lax.rem(d + k, groups),
        )

    def stage_a(n):
        r, s = n // S, lax.rem(n, S)
        slot, cslot, oslot = lax.rem(n, W_SLOTS), lax.rem(n, C_SLOTS), lax.rem(n, 2)

        @pl.when(s == 0)
        def _():
            for cp in x_copies(r):
                cp.wait()

        @pl.when(n >= C_SLOTS)
        def _():
            c_copy(n - C_SLOTS).wait_send()

        copies = w_copies(n)
        for p in range(2):
            copies[p].wait()
            csend[cslot, p] = jnp.dot(
                xbuf[r], wbuf[slot, p], preferred_element_type=f32
            ).astype(bf16)
        @pl.when(n == 0)
        def _():
            pl.semaphore_wait(barrier, groups + 1)

        c_copy(n).start()
        for p in range(2):
            copies[2 + p].wait()
            own[oslot, p] = jnp.dot(xbuf[r], wbuf[slot, 2 + p], preferred_element_type=f32)

        @pl.when(n + W_SLOTS < N)
        def _():
            for cp in w_copies(n + W_SLOTS):
                cp.start()

        @pl.when(s == 1)
        def _():
            for j in range(tiles):
                rows = lax.broadcasted_iota(jnp.int32, (sub, HEAD), 0) + r * sub
                pos = (rows + tile_base[j]).astype(f32)
                angle = pos * freq[0:1, :]
                key = jnp.full((sub, HEAD), is_key, jnp.int32) == 1
                lane = lax.broadcasted_iota(jnp.int32, (sub, HEAD), 1)
                sine = jnp.sin(angle)
                sine = jnp.where(lane < HEAD // 2, -sine, sine)
                at = pl.ds(j * sub, sub)
                cos_t[r, at, :] = jnp.where(key, jnp.cos(angle), 1.0)
                sin_t[r, at, :] = jnp.where(key, sine, 0.0)

    def stage_b(n):
        yslot, oslot = lax.rem(n, Y_SLOTS), lax.rem(n, 2)

        @pl.when(n >= Y_SLOTS)
        def _():
            y_copy(n - Y_SLOTS).wait_send()

        c_copy(n).wait_recv()
        ysend[yslot] = (own[oslot, 0] + crecv[n, 0].astype(f32)).astype(bf16)
        y_copy(n).start()
        mine[yslot] = own[oslot, 1] + crecv[n, 1].astype(f32)

    def stage_c(n):
        s = lax.rem(n, S)
        yslot = lax.rem(n, Y_SLOTS)

        @pl.when(n == 0)
        def _():
            for cp in kv_copies():
                cp.wait()

        @pl.when(s == 0)
        def _():
            kvacc[...] = jnp.zeros_like(kvacc)
            sqacc[...] = jnp.zeros_like(sqacc)

        cols = pl.ds(pl.multiple_of(t * width + s * wc, wc), wc)
        bias = b2f[0:1, cols]
        scale = gf[0:1, cols]
        y_copy(n).wait_recv()
        proj = (mine[yslot] + yrecv[n].astype(f32) + bias).astype(bf16).astype(f32)
        sq = proj * proj
        total = sq[:, 0:128]
        for at in range(128, wc, 128):
            total = total + sq[:, at : at + 128]
        sqacc[...] += total
        u = (proj * scale).astype(bf16)
        at = pl.ds(pl.multiple_of(s * wc, wc), wc)
        for p in range(4):
            kvacc[p] += jnp.dot(u, kvbuf[p, at, :], preferred_element_type=f32)

    def stage_d(r):
        for p in range(2):
            kcsend[r, p] = kvacc[p].astype(bf16)
        kc_copy(r).start()
        row_sum = jnp.sum(sqacc[...], axis=1, keepdims=True)
        sqsend[r] = jnp.broadcast_to(row_sum, (M, 128)).T[0:8, :]
        sqc_copy(r).start()
        kmine[0] = kvacc[2]
        kmine[1] = kvacc[3]

    def stage_e(r):
        kc_copy(r).wait_recv()
        kysend[r] = (kmine[0] + kcrecv[r, 0].astype(f32)).astype(bf16)
        ky_copy(r).start()
        sqc_copy(r).wait_recv()
        sqysend[r] = sqsend[r] + sqcrecv[r]
        sqy_copy(r).start()
        kmine[1] = kmine[1] + kcrecv[r, 1].astype(f32)

    def stage_f(r):
        sqy_copy(r).wait_recv()
        total = (sqysend[r] + sqyrecv[r])[0:1, :]
        norm = lax.rsqrt(jnp.broadcast_to(total, (128, M)).T * (1.0 / model) + EPS)
        ky_copy(r).wait_recv()
        cosine, sine = cos_t[r], sin_t[r]
        heads = []
        for h in range(kc // HEAD):
            at = slice(h * HEAD, (h + 1) * HEAD)
            part = kmine[1, :, at] + kyrecv[r, :, at].astype(f32)
            kb = kvbf[0:1, pl.ds(pl.multiple_of(t * kc + h * HEAD, HEAD), HEAD)]
            v = part * norm + kb
            heads.append(v * cosine + pltpu.roll(v, HEAD // 2, 1) * sine)
        for k in range(groups):
            g = lax.rem(d + k, groups)
            for h in range(kc // HEAD):
                at = slice(h * HEAD, (h + 1) * HEAD)
                picked = jnp.zeros((sub, HEAD), f32)
                for j in range(tiles):
                    hit = jnp.full((sub, HEAD), tile_group[j], jnp.int32) == g
                    picked = jnp.where(hit, heads[h][j * sub : (j + 1) * sub, :], picked)
                asend[r, k, :, at] = picked.astype(bf16)
            if k > 0:
                a_send(r, k).start()
        arecv[d, pl.ds(pl.multiple_of(r * sub, sub), sub), :] = asend[r, 0]

    def step(i, carry):
        @pl.when(i < N)
        def _():
            stage_a(i)

        @pl.when(jnp.logical_and(i >= 1, i <= N))
        def _():
            stage_b(i - 1)

        after_d = i - LAG - E_LAG - (S - 1)
        @pl.when(jnp.logical_and(after_d >= 0, lax.rem(after_d + S * R, S) == 0))
        def _():
            stage_e(after_d // S)

        after_e = after_d - F_LAG
        @pl.when(jnp.logical_and(after_e >= 0, lax.rem(after_e + S * R, S) == 0))
        def _():
            stage_f(after_e // S)

        @pl.when(jnp.logical_and(i >= LAG, i < N + LAG))
        def _():
            n = i - LAG
            stage_c(n)

            @pl.when(lax.rem(n, S) == S - 1)
            def _():
                stage_d(n // S)

        return carry

    lax.fori_loop(0, N + LAG + E_LAG + F_LAG, step, 0)

    for n in range(N - C_SLOTS, N):
        c_copy(jnp.int32(n)).wait_send()
    for n in range(N - Y_SLOTS, N):
        y_copy(jnp.int32(n)).wait_send()
    for r in range(R):
        kc_copy(r).wait_send()
        sqc_copy(r).wait_send()
        ky_copy(r).wait_send()
        sqy_copy(r).wait_send()
        for k in range(1, groups):
            a_send(r, k).wait_send()
    for r in range(R):
        for k in range(1, groups):
            a_recv(r, k).wait_recv()
    for k in range(groups):
        index = lax.rem(first + k, groups)
        block = arecv[index].astype(f32)
        valid = jnp.full(block.shape, count, jnp.int32) > k
        out[pl.ds(k * rows_tile, rows_tile), :] = jnp.where(valid, block, 0.0).astype(bf16)


def fused_body(groups, *args):
    hidden, w, b2, gain, kvw, kvb, tpr, rg, tl = args
    tiles, _, rows_tile, width = hidden.shape
    R, S = ROW_CHUNKS, COL_CHUNKS
    N = R * S
    model = w.shape[1]
    wc = width // S
    sub = rows_tile // R
    M = tiles * sub
    cols = kvw.shape[1]
    kc = cols // 4
    half = HEAD // 2
    freqs = ROPE_BASE ** (-jnp.arange(half, dtype=jnp.float32) * 2.0 / HEAD)
    freqs = jnp.broadcast_to(jnp.concatenate([freqs, freqs])[None, :], (8, HEAD))
    f32, bf16 = jnp.float32, jnp.bfloat16
    any_, vmem, smem = (
        pl.BlockSpec(memory_space=s) for s in (pl.ANY, pltpu.VMEM, pltpu.SMEM)
    )
    V, D = pltpu.VMEM, pltpu.SemaphoreType.DMA
    rows = 2 * tiles * rows_tile
    return pl.pallas_call(
        functools.partial(fused_kernel, groups, tpr.shape[0]),
        out_shape=jax.ShapeDtypeStruct((rows, kc), bf16),
        in_specs=[any_, any_, vmem, vmem, any_, vmem, smem, smem, smem, vmem],
        out_specs=vmem,
        scratch_shapes=[
            V((R, M, width), bf16),
            V((W_SLOTS, 4, width, wc), bf16),
            V((4, width, kc), bf16),
            V((1, model), f32),
            V((1, model), f32),
            V((1, cols), f32),
            V((C_SLOTS, 2, M, wc), bf16),
            V((N, 2, M, wc), bf16),
            V((2, 2, M, wc), f32),
            V((Y_SLOTS, M, wc), bf16),
            V((N, M, wc), bf16),
            V((Y_SLOTS, M, wc), f32),
            V((4, M, kc), f32),
            V((M, 128), f32),
            V((R, 2, M, kc), bf16),
            V((R, 2, M, kc), bf16),
            V((R, M, kc), bf16),
            V((R, M, kc), bf16),
            V((2, M, kc), f32),
            V((R, 8, M), f32),
            V((R, 8, M), f32),
            V((R, 8, M), f32),
            V((R, 8, M), f32),
            V((R, M, HEAD), f32),
            V((R, M, HEAD), f32),
            V((R, groups, sub, kc), bf16),
            V((groups, rows_tile, kc), bf16),
            D((R, tiles)),
            D((W_SLOTS, 4)),
            D((4,)),
            D((C_SLOTS,)),
            D((N,)),
            D((Y_SLOTS,)),
            D((N,)),
            D((2, R)),
            D((2, R)),
            D((2, R)),
            D((2, R)),
            D((R, groups)),
            D((R, groups)),
        ],
        compiler_params=pltpu.CompilerParams(
            collective_id=0, has_side_effects=True, vmem_limit_bytes=63 * 1024 * 1024
        ),
    )(
        hidden.reshape(tiles, rows_tile, width),
        w,
        b2.reshape(1, model),
        gain.reshape(1, model),
        kvw,
        kvb.reshape(1, cols),
        tpr,
        rg,
        tl,
        freqs,
    )


def solution(mesh):
    groups = mesh.shape["dom"]
    fused = mesh.shape["tp"] == 4
    return jax.shard_map(
        functools.partial(fused_body, groups) if fused else body,
        mesh=mesh,
        in_specs=(
            P(None, "dom", None, "tp"),
            P("tp", None),
            P(),
            P(),
            P("tp", None),
            P(),
            P(),
            P(),
            P(),
        ),
        out_specs=P("dom", "tp"),
        check_vma=False,
    )
```

```python
import functools

import jax
import jax.numpy as jnp
from jax import lax
from jax.experimental import pallas as pl
from jax.experimental.pallas import tpu as pltpu
from jax.sharding import PartitionSpec as P

HEAD = 128


EPS = 1e-06
ROPE_BASE = 1000000.0


def tile_plan(tiles_per_request, request_group, text_lengths, tile_count, group_count, rows_tile):
    request_count = tiles_per_request.shape[0]
    ends = jnp.cumsum(tiles_per_request)
    starts = ends - tiles_per_request
    tile_ids = jnp.arange(tile_count, dtype=jnp.int32)
    owner = jnp.sum((ends[None, :] <= tile_ids[:, None]).astype(jnp.int32), axis=1)
    member = (owner[:, None] == jnp.arange(request_count, dtype=jnp.int32)[None, :]).astype(
        jnp.int32
    )
    start_of = jnp.sum(member * starts[None, :], axis=1)
    group_of = jnp.sum(member * request_group[None, :], axis=1)
    text_of = jnp.sum(member * text_lengths[None, :], axis=1)
    group_ids = jnp.arange(group_count, dtype=jnp.int32)
    same_group = (request_group[None, :] == group_ids[:, None]).astype(jnp.int32)
    below_group = (request_group[None, :] < group_ids[:, None]).astype(jnp.int32)
    counts = jnp.sum(same_group * tiles_per_request[None, :], axis=1)
    firsts = jnp.sum(below_group * tiles_per_request[None, :], axis=1)
    first_of = jnp.sum(
        (group_of[:, None] == group_ids[None, :]).astype(jnp.int32) * firsts[None, :], axis=1
    )
    slot_of = tile_ids - first_of
    base_of = text_of + (tile_ids - start_of) * rows_tile
    return (group_of, slot_of, base_of, counts, firsts)


def rotate_heads(values, positions, head_size):
    row_count, col_count = values.shape
    grid = values.reshape(row_count, col_count // head_size, head_size)
    half_size = head_size // 2
    freqs = ROPE_BASE ** (-jnp.arange(half_size, dtype=jnp.float32) * 2.0 / head_size)
    angles = positions.astype(jnp.float32)[:, None] * freqs[None, :]
    cosine = jnp.concatenate([jnp.cos(angles), jnp.cos(angles)], axis=1)[:, None, :]
    sine = jnp.concatenate([jnp.sin(angles), jnp.sin(angles)], axis=1)[:, None, :]
    turned = jnp.concatenate([-grid[..., half_size:], grid[..., :half_size]], axis=-1)
    return (grid * cosine + turned * sine).reshape(row_count, col_count)


def lookup(table, wanted):
    table_ids = jnp.arange(table.shape[0], dtype=jnp.int32)
    hits = (wanted[:, None] == table_ids[None, :]).astype(jnp.int32)
    return jnp.sum(hits * table[None, :], axis=1)


def pick_rows(picker, payload):
    return jnp.dot(picker, payload, preferred_element_type=jnp.float32).astype(jnp.bfloat16)


def finish_cache(summed, kv_bias, positions, lane_index, lane_cols, cache_cols):
    bias_part = lax.dynamic_slice_in_dim(kv_bias, lane_index * lane_cols, lane_cols).astype(
        jnp.float32
    )
    raw = summed + bias_part[None, :]
    turned = rotate_heads(raw, positions, HEAD)
    is_key = lane_index * lane_cols < cache_cols // 2
    return jnp.where(is_key, turned, raw).astype(jnp.bfloat16)


def body(
    hidden,
    fc2_weight,
    fc2_bias,
    norm_gain,
    kv_weight,
    kv_bias,
    tiles_per_request,
    request_group,
    text_lengths,
):
    group_count = lax.axis_size("dom")
    lane_count = lax.axis_size("tp")
    group_index = lax.axis_index("dom")
    lane_index = lax.axis_index("tp")
    local_tiles = hidden.shape[0]
    rows_tile = hidden.shape[2]
    local_width = hidden.shape[3]
    model_width = fc2_weight.shape[1]
    cache_cols = kv_weight.shape[1]
    lane_cols = cache_cols // lane_count
    pre_tiles = 2 * local_tiles
    tile_count = local_tiles * group_count
    group_of, slot_of, base_of, counts, firsts = tile_plan(
        tiles_per_request, request_group, text_lengths, tile_count, group_count, rows_tile
    )
    tile_rows = hidden.reshape(local_tiles * rows_tile, local_width)
    partial_value = jnp.dot(tile_rows, fc2_weight, preferred_element_type=jnp.float32).reshape(
        local_tiles, rows_tile, model_width
    )
    summed_cols = lax.psum_scatter(
        partial_value.astype(jnp.bfloat16), "tp", scatter_dimension=2, tiled=True
    ).astype(jnp.float32)
    bias_part = lax.dynamic_slice_in_dim(fc2_bias, lane_index * local_width, local_width).astype(
        jnp.float32
    )
    gain_part = lax.dynamic_slice_in_dim(norm_gain, lane_index * local_width, local_width).astype(
        jnp.float32
    )
    projected = (summed_cols + bias_part[None, None, :]).astype(jnp.bfloat16)
    widened = projected.astype(jnp.float32)
    squares = lax.psum(jnp.sum(widened * widened, axis=2), "tp")
    scale = lax.rsqrt(squares / model_width + EPS)[..., None]
    normed = (widened * scale * gain_part[None, None, :]).astype(jnp.bfloat16)
    group_ids = jnp.arange(group_count, dtype=jnp.int32)
    mine = jnp.arange(local_tiles, dtype=jnp.int32) * group_count + group_index
    mine_group = lookup(group_of, mine)
    send_picker = (group_ids[:, None] == mine_group[None, :]).astype(jnp.bfloat16)
    slot_ids = jnp.arange(pre_tiles, dtype=jnp.int32)
    my_count = lookup(counts, jnp.full((1,), group_index, jnp.int32))[0]
    my_first = lookup(firsts, jnp.full((1,), group_index, jnp.int32))[0]
    wanted = my_first + slot_ids
    valid = slot_ids < my_count
    source = wanted % group_count
    take_picker = jnp.logical_and(source[:, None] == group_ids[None, :], valid[:, None]).astype(
        jnp.bfloat16
    )
    row_ids = jnp.arange(rows_tile, dtype=jnp.int32)
    partial_kv = jnp.dot(
        normed.reshape(local_tiles * rows_tile, local_width),
        kv_weight,
        preferred_element_type=jnp.float32,
    )
    summed_kv = lax.psum_scatter(
        partial_kv.astype(jnp.bfloat16), "tp", scatter_dimension=1, tiled=True
    ).astype(jnp.float32)
    mine_positions = (lookup(base_of, mine)[:, None] + row_ids[None, :]).reshape(
        local_tiles * rows_tile
    )
    cache = finish_cache(summed_kv, kv_bias, mine_positions, lane_index, lane_cols, cache_cols)
    outgoing = pick_rows(send_picker, cache.reshape(local_tiles, rows_tile * lane_cols))
    arrived = lax.all_to_all(
        outgoing.reshape(group_count, rows_tile, lane_cols),
        "dom",
        split_axis=0,
        concat_axis=0,
        tiled=True,
    )
    placed = pick_rows(take_picker, arrived.reshape(group_count, rows_tile * lane_cols))
    return placed.reshape(pre_tiles * rows_tile, lane_cols)


ROW_CHUNKS = 4
COL_CHUNKS = 8
W_SLOTS = 3
C_SLOTS = 4
Y_SLOTS = 8
LAG = 5
E_LAG = 1
KV_STEPS = (4, 6, 8)
F_LAG = 4


def fused_kernel(
    groups,
    requests,
    x,
    w,
    kvw,
    vecs,
    tpr,
    rg,
    tl,
    freq,
    out,
    xbuf,
    wbuf,
    kvbuf,
    csend,
    crecv,
    own,
    ysend,
    yrecv,
    mine,
    kvacc,
    sqacc,
    kcsend,
    kcrecv,
    kysend,
    kyrecv,
    kmine,
    ubuf,
    sqsend,
    sqcrecv,
    sqysend,
    sqyrecv,
    cos_t,
    sin_t,
    asend,
    arecv,
    xsem,
    wsem,
    kvsem,
    cs_sem,
    cr_sem,
    ys_sem,
    yr_sem,
    ks_sem,
    kr_sem,
    kys_sem,
    kyr_sem,
    as_sem,
    ar_sem,
):
    tiles, rows_tile, width = x.shape
    R, S = ROW_CHUNKS, COL_CHUNKS
    N = R * S
    sub = rows_tile // R
    M = tiles * sub
    model = w.shape[1]
    wc = width // S
    kc = kvw.shape[1] // 4
    kh = kc // 2
    t = lax.axis_index("tp")
    d = lax.axis_index("dom")
    c = lax.rem(t, 2)
    y = t // 2
    sib = t + 1 - 2 * c
    opp = t + 2 - 4 * y
    oy, oc = 1 - y, 1 - c
    owners = (2 * oy + oc, 2 * y + oc, 2 * oy + c, t)
    f32, bf16 = jnp.float32, jnp.bfloat16

    def x_copies(r):
        return [
            pltpu.make_async_copy(
                x.at[j, pl.ds(r * sub, sub), :], xbuf.at[r, pl.ds(j * sub, sub), :], xsem.at[r, j]
            )
            for j in range(tiles)
        ]

    def w_copies(n):
        s = lax.rem(n, S)
        slot = lax.rem(n, W_SLOTS)
        return [
            pltpu.make_async_copy(
                w.at[:, pl.ds(pl.multiple_of(owners[p] * width + s * wc, wc), wc)],
                wbuf.at[slot, p // 2, :, pl.ds(p % 2 * wc, wc)],
                wsem.at[slot, p],
            )
            for p in range(4)
        ]

    def kv_copies():
        return [
            pltpu.make_async_copy(
                kvw.at[:, pl.ds(pl.multiple_of(owners[p] * kc, kc), kc)],
                kvbuf.at[p],
                kvsem.at[p],
            )
            for p in range(4)
        ]

    for cp in x_copies(0):
        cp.start()
    for cp in w_copies(jnp.int32(0)):
        cp.start()

    barrier = pltpu.get_barrier_semaphore()
    pl.semaphore_signal(barrier, inc=1, device_id={"tp": sib}, device_id_type=pl.DeviceIdType.MESH)
    pl.semaphore_signal(barrier, inc=1, device_id={"tp": opp}, device_id_type=pl.DeviceIdType.MESH)
    for k in range(1, groups):
        pl.semaphore_signal(
            barrier,
            inc=1,
            device_id={"dom": lax.rem(d + k, groups)},
            device_id_type=pl.DeviceIdType.MESH,
        )

    tile_group = []
    tile_base = []
    for j in range(tiles):
        tid = j * groups + d
        end = jnp.int32(0)
        grp = jnp.int32(0)
        base = jnp.int32(0)
        for q in range(requests):
            start = end
            end = end + tpr[q]
            hit = jnp.logical_and(start <= tid, tid < end)
            grp = grp + jnp.where(hit, rg[q], 0)
            base = base + jnp.where(hit, tl[q] + (tid - start) * rows_tile, 0)
        tile_group.append(grp)
        tile_base.append(base)
    first = jnp.int32(0)
    count = jnp.int32(0)
    for q in range(requests):
        first = first + jnp.where(rg[q] < d, tpr[q], 0)
        count = count + jnp.where(rg[q] == d, tpr[q], 0)
    is_key = (t * kc < 2 * kc).astype(jnp.int32)

    def remote(src, dst, send, recv, axis, target):
        return pltpu.make_async_remote_copy(
            src_ref=src,
            dst_ref=dst,
            send_sem=send,
            recv_sem=recv,
            device_id={axis: target},
            device_id_type=pl.DeviceIdType.MESH,
        )

    def c_copy(n):
        slot = lax.rem(n, C_SLOTS)
        return remote(csend.at[slot], crecv.at[n], cs_sem.at[slot], cr_sem.at[n], "tp", sib)

    def y_copy(n):
        slot = lax.rem(n, Y_SLOTS)
        return remote(ysend.at[slot], yrecv.at[n], ys_sem.at[slot], yr_sem.at[n], "tp", opp)

    def kc_copy(r):
        return remote(kcsend.at[r], kcrecv.at[r], ks_sem.at[0, r], kr_sem.at[0, r], "tp", sib)

    def sqc_copy(r):
        return remote(sqsend.at[r], sqcrecv.at[r], ks_sem.at[1, r], kr_sem.at[1, r], "tp", sib)

    def ky_copy(r, part):
        return remote(
            kysend.at[r, part],
            kyrecv.at[r, part],
            kys_sem.at[part, r],
            kyr_sem.at[part, r],
            "tp",
            opp,
        )

    def sqy_copy(r):
        return remote(sqysend.at[r], sqyrecv.at[r], kys_sem.at[2, r], kyr_sem.at[2, r], "tp", opp)

    def a_copy(r, k, part, origin):
        return remote(
            asend.at[r, part, k],
            arecv.at[part, origin, pl.ds(pl.multiple_of(r * sub, sub), sub), :],
            as_sem.at[r, part, k],
            ar_sem.at[r, part, k],
            "dom",
            lax.rem(d + k, groups),
        )

    def a_send(r, k, part):
        return a_copy(r, k, part, d)

    def a_recv(r, k, part):
        return a_copy(r, k, part, lax.rem(d + groups - k, groups))

    def stage_a(n):
        r, s = n // S, lax.rem(n, S)
        slot, cslot, oslot = lax.rem(n, W_SLOTS), lax.rem(n, C_SLOTS), lax.rem(n, 2)

        @pl.when(s == 0)
        def _():
            for cp in x_copies(r):
                cp.wait()

        @pl.when(n >= C_SLOTS)
        def _():
            c_copy(n - C_SLOTS).wait_send()

        copies = w_copies(n)
        for p in range(2):
            copies[p].wait()
        away = jnp.dot(xbuf[r], wbuf[slot, 0], preferred_element_type=f32).astype(bf16)
        for p in range(2):
            csend[cslot, p] = away[:, p * wc : (p + 1) * wc]
        @pl.when(n == 0)
        def _():
            pl.semaphore_wait(barrier, groups + 1)

        c_copy(n).start()

        @pl.when(n == 0)
        def _():
            for cp in w_copies(jnp.int32(1)):
                cp.start()

        for p in range(2):
            copies[2 + p].wait()
        home = jnp.dot(xbuf[r], wbuf[slot, 1], preferred_element_type=f32)
        for p in range(2):
            own[oslot, p] = home[:, p * wc : (p + 1) * wc]

        @pl.when(n == 0)
        def _():
            for k in range(2, W_SLOTS):
                for cp in w_copies(jnp.int32(k)):
                    cp.start()

        @pl.when(n + W_SLOTS < N)
        def _():
            for cp in w_copies(n + W_SLOTS):
                cp.start()

        @pl.when(n == 1)
        def _():
            for cp in kv_copies():
                cp.start()
            for k in range(1, R):
                for cp in x_copies(k):
                    cp.start()

        @pl.when(s == 1)
        def _():
            for j in range(tiles):
                rows = lax.broadcasted_iota(jnp.int32, (sub, HEAD), 0) + r * sub
                pos = (rows + tile_base[j]).astype(f32)
                angle = pos * freq[0:1, :]
                key = jnp.full((sub, HEAD), is_key, jnp.int32) == 1
                lane = lax.broadcasted_iota(jnp.int32, (sub, HEAD), 1)
                sine = jnp.sin(angle)
                sine = jnp.where(lane < HEAD // 2, -sine, sine)
                at = pl.ds(j * sub, sub)
                cos_t[r, at, :] = jnp.where(key, jnp.cos(angle), 1.0)
                sin_t[r, at, :] = jnp.where(key, sine, 0.0)

    def stage_b(n):
        yslot, oslot = lax.rem(n, Y_SLOTS), lax.rem(n, 2)

        @pl.when(n >= Y_SLOTS)
        def _():
            y_copy(n - Y_SLOTS).wait_send()

        c_copy(n).wait_recv()
        ysend[yslot] = (own[oslot, 0] + crecv[n, 0].astype(f32)).astype(bf16)
        y_copy(n).start()
        mine[yslot] = own[oslot, 1] + crecv[n, 1].astype(f32)

    def stage_c(n):
        s = lax.rem(n, S)
        yslot = lax.rem(n, Y_SLOTS)

        @pl.when(n == 0)
        def _():
            for cp in kv_copies():
                cp.wait()

        cols = pl.ds(pl.multiple_of(t * width + s * wc, wc), wc)
        gcols = pl.ds(pl.multiple_of(model + t * width + s * wc, wc), wc)
        bias = vecs[0:1, cols]
        scale = vecs[0:1, gcols]
        y_copy(n).wait_recv()
        proj = (mine[yslot] + yrecv[n].astype(f32) + bias).astype(bf16).astype(f32)
        sq = proj * proj
        total = sq[:, 0:128]
        for at in range(128, wc, 128):
            total = total + sq[:, at : at + 128]

        @pl.when(s == 0)
        def _():
            sqacc[...] = jnp.zeros_like(sqacc)

        sqacc[...] += total
        ubuf[s] = (proj * scale).astype(bf16)

        low = 0
        for high in KV_STEPS:

            @pl.when(s == high - 1)
            def _(low=low, high=high):
                u = jnp.concatenate([ubuf[q] for q in range(low, high)], axis=1)
                for p in range(4):
                    more = jnp.dot(
                        u, kvbuf[p, low * wc : high * wc, :], preferred_element_type=f32
                    )
                    kvacc[p] = more if low == 0 else kvacc[p] + more

            low = high

    def stage_d(r):
        for p in range(2):
            kcsend[r, p] = kvacc[p].astype(bf16)
        kc_copy(r).start()
        row_sum = jnp.sum(sqacc[...], axis=1, keepdims=True)
        sqsend[r] = jnp.broadcast_to(row_sum, (M, 128)).T[0:8, :]
        sqc_copy(r).start()

    def stage_e(r):
        kc_copy(r).wait_recv()
        for part in range(2):
            at = slice(part * kh, (part + 1) * kh)
            kysend[r, part] = (kvacc[2, :, at] + kcrecv[r, 0, :, at].astype(f32)).astype(bf16)
            ky_copy(r, part).start()
            if part == 0:
                sqc_copy(r).wait_recv()
                sqysend[r] = sqsend[r] + sqcrecv[r]
                sqy_copy(r).start()
        kmine[...] = kvacc[3] + kcrecv[r, 1].astype(f32)

    def stage_f(r):
        cosine, sine = cos_t[r], sin_t[r]
        rows = pl.ds(pl.multiple_of(r * sub, sub), sub)
        norm = None
        for part in range(2):
            ky_copy(r, part).wait_recv()
            if part == 0:
                sqy_copy(r).wait_recv()
                total = (sqysend[r] + sqyrecv[r])[0:1, :]
                norm = lax.rsqrt(jnp.broadcast_to(total, (128, M)).T * (1.0 / model) + EPS)
            heads = []
            for h in range(kh // HEAD):
                here = slice(h * HEAD, (h + 1) * HEAD)
                at = slice(part * kh + h * HEAD, part * kh + (h + 1) * HEAD)
                sums = kmine[:, at] + kyrecv[r, part, :, here].astype(f32)
                start = pl.multiple_of(2 * model + t * kc + part * kh + h * HEAD, HEAD)
                v = sums * norm + vecs[0:1, pl.ds(start, HEAD)]
                heads.append(v * cosine + pltpu.roll(v, HEAD // 2, 1) * sine)
            for k in list(range(1, groups)) + [0]:
                g = lax.rem(d + k, groups)
                for h in range(kh // HEAD):
                    here = slice(h * HEAD, (h + 1) * HEAD)
                    picked = jnp.zeros((sub, HEAD), f32)
                    for j in range(tiles):
                        hit = jnp.full((sub, HEAD), tile_group[j], jnp.int32) == g
                        picked = jnp.where(hit, heads[h][j * sub : (j + 1) * sub, :], picked)
                    asend[r, part, k, :, here] = picked.astype(bf16)
                if k > 0:
                    a_send(r, k, part).start()
            arecv[part, d, rows, :] = asend[r, part, 0]

    def step(i, carry):
        @pl.when(i < N)
        def _():
            stage_a(i)

        @pl.when(jnp.logical_and(i >= 1, i <= N))
        def _():
            stage_b(i - 1)

        after_d = i - LAG - E_LAG - (S - 1)
        @pl.when(jnp.logical_and(after_d >= 0, lax.rem(after_d + S * R, S) == 0))
        def _():
            stage_e(after_d // S)

        after_e = after_d - F_LAG
        @pl.when(jnp.logical_and(after_e >= 0, lax.rem(after_e + S * R, S) == 0))
        def _():
            stage_f(after_e // S)

        @pl.when(jnp.logical_and(i >= LAG, i < N + LAG))
        def _():
            n = i - LAG
            stage_c(n)

            @pl.when(lax.rem(n, S) == S - 1)
            def _():
                stage_d(n // S)

        return carry

    lax.fori_loop(0, N + LAG + E_LAG + F_LAG, step, 0)

    for n in range(N - C_SLOTS, N):
        c_copy(jnp.int32(n)).wait_send()
    for n in range(N - Y_SLOTS, N):
        y_copy(jnp.int32(n)).wait_send()
    for r in range(R):
        kc_copy(r).wait_send()
        sqc_copy(r).wait_send()
        sqy_copy(r).wait_send()
        for part in range(2):
            ky_copy(r, part).wait_send()
            for k in range(1, groups):
                a_send(r, k, part).wait_send()
    for r in range(R):
        for part in range(2):
            for k in range(1, groups):
                a_recv(r, k, part).wait_recv()
    for k in range(groups):
        index = lax.rem(first + k, groups)
        for part in range(2):
            block = arecv[part, index].astype(f32)
            valid = jnp.full(block.shape, count, jnp.int32) > k
            at = slice(part * kh, (part + 1) * kh)
            out[pl.ds(k * rows_tile, rows_tile), at] = jnp.where(valid, block, 0.0).astype(bf16)


def fused_body(groups, *args):
    hidden, w, b2, gain, kvw, kvb, tpr, rg, tl = args
    tiles, _, rows_tile, width = hidden.shape
    R, S = ROW_CHUNKS, COL_CHUNKS
    N = R * S
    model = w.shape[1]
    wc = width // S
    sub = rows_tile // R
    M = tiles * sub
    cols = kvw.shape[1]
    kc = cols // 4
    kh = kc // 2
    half = HEAD // 2
    freqs = ROPE_BASE ** (-jnp.arange(half, dtype=jnp.float32) * 2.0 / HEAD)
    freqs = jnp.broadcast_to(jnp.concatenate([freqs, freqs])[None, :], (8, HEAD))
    f32, bf16 = jnp.float32, jnp.bfloat16
    any_, vmem, smem = (
        pl.BlockSpec(memory_space=s) for s in (pl.ANY, pltpu.VMEM, pltpu.SMEM)
    )
    V, D = pltpu.VMEM, pltpu.SemaphoreType.DMA
    rows = 2 * tiles * rows_tile
    return pl.pallas_call(
        functools.partial(fused_kernel, groups, tpr.shape[0]),
        out_shape=jax.ShapeDtypeStruct((rows, kc), bf16),
        in_specs=[any_, any_, any_, vmem, smem, smem, smem, vmem],
        out_specs=vmem,
        scratch_shapes=[
            V((R, M, width), bf16),
            V((W_SLOTS, 2, width, 2 * wc), bf16),
            V((4, width, kc), bf16),
            V((C_SLOTS, 2, M, wc), bf16),
            V((N, 2, M, wc), bf16),
            V((2, 2, M, wc), f32),
            V((Y_SLOTS, M, wc), bf16),
            V((N, M, wc), bf16),
            V((Y_SLOTS, M, wc), f32),
            V((4, M, kc), f32),
            V((M, 128), f32),
            V((R, 2, M, kc), bf16),
            V((R, 2, M, kc), bf16),
            V((R, 2, M, kh), bf16),
            V((R, 2, M, kh), bf16),
            V((M, kc), f32),
            V((S, M, wc), bf16),
            V((R, 8, M), f32),
            V((R, 8, M), f32),
            V((R, 8, M), f32),
            V((R, 8, M), f32),
            V((R, M, HEAD), f32),
            V((R, M, HEAD), f32),
            V((R, 2, groups, sub, kh), bf16),
            V((2, groups, rows_tile, kh), bf16),
            D((R, tiles)),
            D((W_SLOTS, 4)),
            D((4,)),
            D((C_SLOTS,)),
            D((N,)),
            D((Y_SLOTS,)),
            D((N,)),
            D((2, R)),
            D((2, R)),
            D((3, R)),
            D((3, R)),
            D((R, 2, groups)),
            D((R, 2, groups)),
        ],
        compiler_params=pltpu.CompilerParams(
            collective_id=0, has_side_effects=True, vmem_limit_bytes=63 * 1024 * 1024
        ),
    )(
        hidden.reshape(tiles, rows_tile, width),
        w,
        kvw,
        jnp.concatenate([b2, gain, kvb]).astype(f32).reshape(1, 2 * model + cols),
        tpr,
        rg,
        tl,
        freqs,
    )


def solution(mesh):
    groups = mesh.shape["dom"]
    fused = mesh.shape["tp"] == 4
    return jax.shard_map(
        functools.partial(fused_body, groups) if fused else body,
        mesh=mesh,
        in_specs=(
            P(None, "dom", None, "tp"),
            P("tp", None),
            P(),
            P(),
            P("tp", None),
            P(),
            P(),
            P(),
            P(),
        ),
        out_specs=P("dom", "tp"),
        check_vma=False,
    )
```
